32 devices in a mesh: leaf: 16 (over z, y, x), group: 2 (over core).
Axes of the slice: x: 2, y: 2, z: 4, core: 2. Of those that a mesh axis runs over, the one named last changes fastest.
Arguments:
- low_solved: float32 [16384, 256], P(('group', 'leaf')), may hold values from -4 to 4, as said below
- low_basis: float32 [16384, 256], P(('group', 'leaf')), may hold values from -0.002734375 to 0.002734375, as said below
- upper_solved: float32 [16384, 512], P(('group', 'leaf')), may hold values from -4 to 4, as said below
- upper_basis: float32 [16384, 256], P(('group', 'leaf')), may hold values from -0.0016572815 to 0.0016572815, as said below
Outputs:
- pair_solved: float32 [16384, 256], P(('group', 'leaf'))
- next_solved: float32 [16384, 256], P(('group', 'leaf'))
The draws below stay inside these ranges and needn't reach their ends.
Inputs may be any that keep to these rules, and one draw needn't show every extreme that they name: `low_solved`: independent entries of mean zero. `low_basis`: independent entries of mean zero. `upper_solved`: independent entries of mean zero. `upper_basis`: independent entries of mean zero.
All inputs are finite; a program needn't handle non-finite values.
Results may differ from the reference program's by a relative error of at most 0.0003.
Values sent between devices are 32-bit elements; how exact they have to be, the bound alone decides.
No kernel may reach another device: no remote copies, remote signals or barrier semaphores. Data moves between devices by JAX's collectives and lax.ppermute only.
A program may use at most 64 MiB of HBM per device.

```python
import jax
import jax.numpy as jnp
from jax import lax

RANK = 256
ITERS = 4
HALF_ROWS = 4096
GROUP_ROWS = 8192
TOTAL_ROWS = 16384
N_GROUP = 2


def spread_draw(key, shape, scale):
    return jnp.clip(jax.random.normal(key, shape, jnp.float32), -4.0, 4.0) * scale


def draw_low_solved(key, part):
    return spread_draw(key, (TOTAL_ROWS, RANK), 1.0)


def draw_low_basis(key, part):
    return spread_draw(key, (TOTAL_ROWS, RANK), 0.7 / (RANK * HALF_ROWS) ** 0.5)


def draw_upper_solved(key, part):
    return spread_draw(key, (TOTAL_ROWS, 2 * RANK), 1.0)


def draw_upper_basis(key, part):
    return spread_draw(key, (TOTAL_ROWS, RANK), 0.6 / (RANK * GROUP_ROWS) ** 0.5)


def setup_inputs(seed: int = 0) -> dict:
    seeds = jax.random.split(jax.random.key(seed), 5)
    return {
        "low_solved": draw_low_solved(jax.random.fold_in(seeds[4], 71), 0),
        "low_basis": draw_low_basis(jax.random.fold_in(seeds[4], 71), 0),
        "upper_solved": draw_upper_solved(jax.random.fold_in(seeds[4], 71), 0),
        "upper_basis": draw_upper_basis(jax.random.fold_in(seeds[4], 71), 0),
    }


def product(left, right):
    return jnp.dot(left, right, precision=lax.Precision.HIGHEST, preferred_element_type=jnp.float32)


def transposed_product(left, right):
    return lax.dot_general(left, right, (((0,), (0,)), ((), ())), precision=lax.Precision.HIGHEST, preferred_element_type=jnp.float32)


def jacobi(couple_first, rhs_first, couple_second, rhs_second):
    update_first = jnp.zeros(rhs_second.shape, jnp.float32)
    update_second = jnp.zeros(rhs_first.shape, jnp.float32)
    for sweep_index in range(ITERS):
        update_first, update_second = rhs_second - product(couple_second, update_second), rhs_first - product(couple_first, update_first)
    return update_first, update_second


def level_group(y_halves, v_halves, z_halves):
    totals = []
    for half_index in range(2):
        joined = jnp.concatenate([y_halves[half_index], z_halves[half_index]], axis=1)
        totals.append(transposed_product(v_halves[half_index], joined))
    update_first, update_second = jacobi(totals[0][:, :RANK], totals[0][:, RANK:], totals[1][:, :RANK], totals[1][:, RANK:])
    middle_first = z_halves[0] - product(y_halves[0], update_first)
    middle_second = z_halves[1] - product(y_halves[1], update_second)
    return jnp.stack([middle_first, middle_second])


def per_pair(pieces):
    y_pair, v_pair, z_pair, w_pair = pieces
    middles = []
    blocks = []
    for group_index in range(2):
        middle = level_group(y_pair[group_index], v_pair[group_index], z_pair[group_index])
        middles.append(middle)
        blocks.append(transposed_product(w_pair[group_index, 0], middle[0]) + transposed_product(w_pair[group_index, 1], middle[1]))
    pair_first, pair_second = jacobi(blocks[0][:, :RANK], blocks[0][:, RANK:], blocks[1][:, :RANK], blocks[1][:, RANK:])
    updates = [pair_first, pair_second]
    solved_rows = []
    next_rows = []
    for group_index in range(2):
        middle = middles[group_index]
        solved = middle[:, :, :RANK]
        nexts = middle[:, :, RANK:] - jnp.stack([product(solved[0], updates[group_index]), product(solved[1], updates[group_index])])
        solved_rows.append(solved)
        next_rows.append(nexts)
    return jnp.stack(solved_rows), jnp.stack(next_rows)


def reference(low_solved, low_basis, upper_solved, upper_basis):
    pairs = N_GROUP // 2
    def split_rows(array):
        return array.reshape(pairs, 2, 2, HALF_ROWS, array.shape[1])
    solved, nexts = lax.map(per_pair, (split_rows(low_solved), split_rows(low_basis), split_rows(upper_solved), split_rows(upper_basis)))
    return solved.reshape(TOTAL_ROWS, RANK), nexts.reshape(TOTAL_ROWS, RANK)
```

```python
import jax
import jax.numpy as jnp
from jax import lax
from jax.sharding import PartitionSpec as P

ITERS = 4


def flip(x, axis, bit):
    return lax.ppermute(x, axis, [(i, i ^ (1 << bit)) for i in range(lax.axis_size(axis))])


def product(left, right):
    return jnp.dot(left, right, precision=lax.Precision.HIGHEST, preferred_element_type=jnp.float32)


def transposed_product(left, right):
    return lax.dot_general(
        left,
        right,
        (((0,), (0,)), ((), ())),
        precision=lax.Precision.HIGHEST,
        preferred_element_type=jnp.float32,
    )


def jacobi(couple_first, rhs_first, couple_second, rhs_second):
    update_first = rhs_second
    update_second = rhs_first
    for sweep_index in range(ITERS - 1):
        update_first, update_second = (
            rhs_second - product(couple_second, update_second),
            rhs_first - product(couple_first, update_first),
        )
    return (update_first, update_second)


def scatter_sums(pieces, bits, own):
    order = [[(p + t) % bits for t in range(bits)] for p in range(len(pieces))]
    left = [list(reversed(range(bits))) for _ in pieces]
    for t in range(bits):
        sends, keeps = [], []
        for p, piece in enumerate(pieces):
            bit = order[p][t]
            dim = 1 + left[p].index(bit)
            left[p].remove(bit)
            sends.append(lax.dynamic_index_in_dim(piece, 1 - own[bit], dim, keepdims=False))
            keeps.append(lax.dynamic_index_in_dim(piece, own[bit], dim, keepdims=False))
        got = [flip(s, "leaf", order[p][t]) for p, s in enumerate(sends)]
        pieces = [k + g for k, g in zip(keeps, got)]
    return pieces


def gather_blocks(pieces, bits, own):
    have = [[] for _ in pieces]
    for t in range(bits):
        got = [flip(s, "leaf", (p + t) % bits) for p, s in enumerate(pieces)]
        grown = []
        for p in range(len(pieces)):
            bit = (p + t) % bits
            low = jnp.where(own[bit] == 0, pieces[p], got[p])
            high = jnp.where(own[bit] == 0, got[p], pieces[p])
            place = sum(1 for b in have[p] if b > bit)
            have[p].insert(place, bit)
            grown.append(jnp.stack([low, high], axis=1 + place))
        pieces = grown
    return [p.reshape(p.shape[0], -1, p.shape[-1]) for p in pieces]


def body(low_solved, low_basis, upper_solved, upper_basis):
    rank = low_solved.shape[1]
    leaves = lax.axis_size("leaf")
    bits = leaves.bit_length() - 2
    blocks = 1 << bits
    index = lax.axis_index("leaf")
    half = index // blocks
    own = [(index >> b) & 1 for b in range(bits)]
    basis = jnp.concatenate([low_basis, upper_basis], axis=1)
    panels = [low_solved, upper_solved[:, :rank], upper_solved[:, rank:]]
    local = [transposed_product(basis, panel) for panel in panels]
    local = [x.reshape([2] + [2] * bits + [rank // blocks, rank]) for x in local]
    sums = scatter_sums(local, bits, own)
    mine = [x[0] for x in sums]
    theirs = [flip(x, "leaf", bits) for x in mine]
    both = [
        jnp.stack([jnp.where(half == 0, m, t), jnp.where(half == 0, t, m)])
        for m, t in zip(mine, theirs)
    ]
    couple, rhs_low, rhs_high = gather_blocks(both, bits, own)
    rhs = jnp.concatenate([rhs_low, rhs_high], axis=2)
    update_first, update_second = jacobi(couple[0], rhs[0], couple[1], rhs[1])
    own_update = jnp.where(half == 0, update_first, update_second)
    rows = [
        sums[1 + i][1] - product(sums[0][1], own_update[:, i * rank : (i + 1) * rank])
        for i in range(2)
    ]
    rows = [x + flip(x, "leaf", bits) for x in rows]
    group_total = gather_blocks([x[None] for x in rows], bits, own)
    group_total = jnp.concatenate([x[0] for x in group_total], axis=1)
    sibling = flip(group_total, "group", 0)
    middle = upper_solved - product(low_solved, own_update)
    pair_solved = middle[:, :rank]
    parity = lax.axis_index("group") % 2
    first_group = jnp.where(parity == 0, group_total, sibling)
    second_group = jnp.where(parity == 0, sibling, group_total)
    pair_first, pair_second = jacobi(
        first_group[:, :rank],
        first_group[:, rank:],
        second_group[:, :rank],
        second_group[:, rank:],
    )
    pair_update = jnp.where(parity == 0, pair_first, pair_second)
    next_solved = middle[:, rank:] - product(pair_solved, pair_update)
    return (pair_solved, next_solved)


def solution(mesh):
    spec = P(("group", "leaf"), None)
    return jax.shard_map(
        body,
        mesh=mesh,
        in_specs=(spec, spec, spec, spec),
        out_specs=(spec, spec),
        check_vma=False,
    )
```

```python
import jax
import jax.numpy as jnp
from jax import lax
from jax.sharding import PartitionSpec as P

ITERS = 4


def flip(x, axis, bit):
    return lax.ppermute(x, axis, [(i, i ^ (1 << bit)) for i in range(lax.axis_size(axis))])


def product(left, right):
    return jnp.dot(left, right, precision=lax.Precision.HIGHEST, preferred_element_type=jnp.float32)


def transposed_product(left, right):
    return lax.dot_general(
        left,
        right,
        (((0,), (0,)), ((), ())),
        precision=lax.Precision.HIGHEST,
        preferred_element_type=jnp.float32,
    )


def jacobi(couple_first, rhs_first, couple_second, rhs_second):
    update_first = rhs_second
    update_second = rhs_first
    for sweep_index in range(ITERS - 1):
        update_first, update_second = (
            rhs_second - product(couple_second, update_second),
            rhs_first - product(couple_first, update_first),
        )
    return (update_first, update_second)


def swap_blocks(x, blocks):
    groups = [list(range(blocks)), list(range(blocks, 2 * blocks))]
    return lax.all_to_all(x, "leaf", 0, 0, axis_index_groups=groups)


def body(low_solved, low_basis, upper_solved, upper_basis):
    rank = low_solved.shape[1]
    leaves = lax.axis_size("leaf")
    bits = leaves.bit_length() - 2
    blocks = 1 << bits
    index = lax.axis_index("leaf")
    half = index // blocks
    joined = jnp.concatenate([low_solved, upper_solved], axis=1)
    low_terms = transposed_product(low_basis, joined).reshape(blocks, rank // blocks, 3 * rank)
    low_parts = swap_blocks(low_terms, blocks)
    upper_terms = transposed_product(upper_basis, joined).reshape(blocks, rank // blocks, 3 * rank)
    upper_parts = swap_blocks(upper_terms, blocks)
    mine = jnp.sum(low_parts, axis=0)
    theirs = flip(mine, "leaf", bits)
    both = jnp.stack([jnp.where(half == 0, mine, theirs), jnp.where(half == 0, theirs, mine)])
    low = swap_blocks(jnp.broadcast_to(both, (blocks,) + both.shape), blocks)
    low = low.transpose(1, 0, 2, 3).reshape(2, rank, 3 * rank)
    update_first, update_second = jacobi(
        low[0, :, :rank], low[0, :, rank:], low[1, :, :rank], low[1, :, rank:]
    )
    own_update = jnp.where(half == 0, update_first, update_second)
    upper = jnp.sum(upper_parts, axis=0)
    rows = upper[:, rank:] - product(upper[:, :rank], own_update)
    rows = rows + flip(rows, "leaf", bits)
    group_total = swap_blocks(jnp.broadcast_to(rows, (blocks,) + rows.shape), blocks)
    group_total = group_total.reshape(rank, 2 * rank)
    sibling = flip(group_total, "group", 0)
    middle = upper_solved - product(low_solved, own_update)
    pair_solved = middle[:, :rank]
    parity = lax.axis_index("group") % 2
    first_group = jnp.where(parity == 0, group_total, sibling)
    second_group = jnp.where(parity == 0, sibling, group_total)
    pair_first, pair_second = jacobi(
        first_group[:, :rank],
        first_group[:, rank:],
        second_group[:, :rank],
        second_group[:, rank:],
    )
    pair_update = jnp.where(parity == 0, pair_first, pair_second)
    next_solved = middle[:, rank:] - product(pair_solved, pair_update)
    return (pair_solved, next_solved)


def solution(mesh):
    spec = P(("group", "leaf"), None)
    return jax.shard_map(
        body,
        mesh=mesh,
        in_specs=(spec, spec, spec, spec),
        out_specs=(spec, spec),
        check_vma=False,
    )
```

```python
import functools

import jax
import jax.numpy as jnp
from jax import lax
from jax.experimental import pallas as pl
from jax.experimental.pallas import tpu as pltpu
from jax.sharding import PartitionSpec as P

AXES = ("leaf", "group")


def axis_order(chain, core, bits, stage):
    if chain == "low":
        first = core
    else:
        first = 2
    order = [(first + t) % bits for t in range(bits)]
    return order if stage == "scatter" else order[::-1]


def relative_bits(order, r, first_is_high):
    bits = len(order)
    out = 0
    for t in range(bits):
        place = bits - 1 - t if first_is_high else t
        if (r >> place) & 1:
            out |= 1 << order[t]
    return out


def step(x, chain, t, bits, stage):
    leaves, groups = lax.axis_size("leaf"), lax.axis_size("group")
    pairs = []
    for leaf in range(leaves):
        for group in range(groups):
            bit = axis_order(chain, group % 2, bits, stage)[t]
            pairs.append((leaf * groups + group, (leaf ^ (1 << bit)) * groups + group))
    return lax.ppermute(x, AXES, pairs)


def flip(x, axis, bit):
    return lax.ppermute(x, axis, [(i, i ^ (1 << bit)) for i in range(lax.axis_size(axis))])


def split(x):
    high = x.astype(jnp.bfloat16)
    low = (x - high.astype(jnp.float32)).astype(jnp.bfloat16)
    return high, low


def dot3(left, right, dims=(((1,), (0,)), ((), ()))):
    dot = functools.partial(
        lax.dot_general, dimension_numbers=dims, preferred_element_type=jnp.float32
    )
    return dot(left[0], right[0]) + (dot(left[0], right[1]) + dot(left[1], right[0]))


def block_of(r, chain, bits, stage):
    orders = [axis_order(chain, core, bits, stage) for core in range(2)]
    moves = [relative_bits(order, r, stage == "scatter") for order in orders]
    own = lax.rem(lax.axis_index("leaf"), 1 << bits)
    core = lax.rem(lax.axis_index("group"), 2)
    return lax.bitwise_xor(own, jnp.where(core == 0, moves[0], moves[1]))


def local_kernel(chain, bits, basis_ref, y_ref, z_ref, send_ref, keep_ref, sums):
    rank = y_ref.shape[1]
    blocks = 1 << bits
    rows = rank // blocks
    dims = (((0,), (0,)), ((), ()))
    basis = split(basis_ref[...])
    sums[:, :rank] = dot3(basis, split(y_ref[...]), dims)
    sums[:, rank:] = dot3(basis, split(z_ref[...]), dims)
    for r in range(blocks):
        start = pl.multiple_of(block_of(r, chain, bits, "scatter") * rows, rows)
        target = send_ref if r >= blocks // 2 else keep_ref
        target[r % (blocks // 2)] = sums[pl.ds(start, rows), :]


def place(parts, chain, bits, target):
    blocks = 1 << bits
    rows = target.shape[-2] // blocks
    for r in range(blocks):
        start = pl.multiple_of(block_of(r, chain, bits, "gather") * rows, rows)
        piece = parts[r // (blocks // 2)][r % (blocks // 2)]
        if len(target.shape) == 3:
            target[:, pl.ds(start, rows), :] = piece
        else:
            target[pl.ds(start, rows), :] = piece


def solve_kernel(bits, first_ref, second_ref, update_ref, terms):
    rank = update_ref.shape[1]
    place((first_ref, second_ref), "low", bits, terms)
    couples = [split(terms[i, :, :rank]) for i in range(2)]
    for i in range(2):
        mine, other = couples[i], couples[1 - i]
        start = terms[1 - i, :, rank:] - dot3(other, split(terms[i, :, rank:]))
        update_ref[i] = start + dot3(other, split(dot3(mine, split(start))))


def total_kernel(bits, first_ref, second_ref, update_ref, total_ref, terms):
    rank = total_ref.shape[0]
    place((first_ref, second_ref), "high", bits, terms)
    total = terms[:, 2 * rank :]
    for i in range(2):
        total = total - dot3(split(terms[:, i * rank : (i + 1) * rank]), split(update_ref[i]))
    total_ref[...] = total


def middle_kernel(y_ref, z_ref, update_ref, pair_ref, next_ref):
    rank = y_ref.shape[1]
    middle = z_ref[...] - dot3(split(y_ref[...]), split(update_ref[0]))
    pair_ref[...] = middle[:, :rank]
    next_ref[...] = middle[:, rank:]


def final_kernel(mine_ref, other_ref, pair_ref, next_ref, out_ref):
    rank = mine_ref.shape[0]
    mine = split(mine_ref[:, :rank])
    other = split(other_ref[:, :rank])
    start = other_ref[:, rank:] - dot3(other, split(mine_ref[:, rank:]))
    update = start + dot3(other, split(dot3(mine, split(start))))
    out_ref[...] = next_ref[...] - dot3(split(pair_ref[...]), split(update))


def run(kernel, shapes, args, scratch=(), flops=0):
    bytes_moved = sum(a.size * 4 for a in args) + sum(4 * s.size for s in shapes)
    return pl.pallas_call(
        kernel,
        out_shape=shapes,
        in_specs=[pl.BlockSpec(memory_space=pltpu.VMEM)] * len(args),
        out_specs=[pl.BlockSpec(memory_space=pltpu.VMEM)] * len(shapes),
        scratch_shapes=list(scratch),
        compiler_params=pltpu.CompilerParams(vmem_limit_bytes=24 * 1024 * 1024),
        cost_estimate=pl.CostEstimate(flops=flops, bytes_accessed=bytes_moved, transcendentals=0),
    )(*args)


def array(*shape):
    return jax.ShapeDtypeStruct(shape, jnp.float32)


def body(low_solved, low_basis, upper_solved, upper_basis):
    depth, rank = low_solved.shape
    leaves = lax.axis_size("leaf")
    bits = leaves.bit_length() - 2
    blocks = 1 << bits
    rows = rank // blocks
    unit = 6 * rank * rank

    def scatter_terms(chain, basis):
        half = array(blocks // 2, rows, 3 * rank)
        return run(
            functools.partial(local_kernel, chain, bits),
            [half, half],
            [basis, low_solved, upper_solved],
            [pltpu.VMEM((rank, 3 * rank), jnp.float32)],
            flops=3 * unit * depth,
        )

    def scatter(chain, send, keep):
        for t in range(bits):
            got = step(send, chain, t, bits, "scatter")
            if t == bits - 1:
                return keep[0] + got[0]
            half = keep.shape[0] // 2
            send = keep[half:] + got[half:]
            keep = keep[:half] + got[:half]

    def gather(chain, x):
        for t in range(bits):
            got = step(x, chain, t, bits, "gather")
            if t == bits - 1:
                return x, got
            x = jnp.concatenate([x, got], axis=0)

    low_mine = scatter("low", *scatter_terms("low", low_basis))
    low_other = flip(low_mine, "leaf", bits)
    low_parts = gather("low", jnp.stack([low_mine, low_other])[None])

    high_mine = scatter("high", *scatter_terms("high", upper_basis))
    high_other = flip(high_mine, "leaf", bits)
    joined = jnp.concatenate(
        [high_mine[:, :rank], high_other[:, :rank], high_mine[:, rank:] + high_other[:, rank:]],
        axis=1,
    )
    high_parts = gather("high", joined[None])

    (update,) = run(
        functools.partial(solve_kernel, bits),
        [array(2, rank, 2 * rank)],
        low_parts,
        [pltpu.VMEM((2, rank, 3 * rank), jnp.float32)],
        flops=12 * unit * rank,
    )
    (total,) = run(
        functools.partial(total_kernel, bits),
        [array(rank, 2 * rank)],
        [*high_parts, update],
        [pltpu.VMEM((rank, 4 * rank), jnp.float32)],
        flops=4 * unit * rank,
    )
    sibling = flip(total, "group", 0)
    pair_solved, next_terms = run(
        middle_kernel,
        [array(depth, rank), array(depth, rank)],
        [low_solved, upper_solved, update],
        flops=2 * unit * depth,
    )
    (next_solved,) = run(
        final_kernel,
        [array(depth, rank)],
        [total, sibling, pair_solved, next_terms],
        flops=3 * unit * rank + unit * depth,
    )
    return pair_solved, next_solved


def solution(mesh):
    spec = P(("group", "leaf"), None)
    return jax.shard_map(
        body,
        mesh=mesh,
        in_specs=(spec, spec, spec, spec),
        out_specs=(spec, spec),
        check_vma=False,
    )
```

```python
import functools

import jax
import jax.numpy as jnp
from jax import lax
from jax.experimental import pallas as pl
from jax.experimental.pallas import tpu as pltpu
from jax.sharding import PartitionSpec as P

AXES = ("leaf", "group")


def axis_order(chain, core, bits, stage):
    pair, rest = [core, 1 - core], list(range(2, bits))
    if chain == "low":
        if stage == "scatter":
            return pair + rest
        return (rest + [1, 0]) if core == 0 else ([0] + rest + [1])
    if stage == "scatter":
        return rest + pair
    return [core] + rest + [1 - core]


def relative_bits(order, r, first_is_high):
    bits = len(order)
    out = 0
    for t in range(bits):
        place = bits - 1 - t if first_is_high else t
        if (r >> place) & 1:
            out |= 1 << order[t]
    return out


def step(x, chain, t, bits, stage):
    leaves, groups = lax.axis_size("leaf"), lax.axis_size("group")
    pairs = []
    for leaf in range(leaves):
        for group in range(groups):
            bit = axis_order(chain, group % 2, bits, stage)[t]
            pairs.append((leaf * groups + group, (leaf ^ (1 << bit)) * groups + group))
    return lax.ppermute(x, AXES, pairs)


def flip(x, axis, bit):
    return lax.ppermute(x, axis, [(i, i ^ (1 << bit)) for i in range(lax.axis_size(axis))])


def split(x):
    high = x.astype(jnp.bfloat16)
    low = (x - high.astype(jnp.float32)).astype(jnp.bfloat16)
    return high, low


def dot3(left, right, dims=(((1,), (0,)), ((), ()))):
    dot = functools.partial(
        lax.dot_general, dimension_numbers=dims, preferred_element_type=jnp.float32
    )
    return dot(left[0], right[0]) + (dot(left[0], right[1]) + dot(left[1], right[0]))


def block_of(r, chain, bits, stage):
    orders = [axis_order(chain, core, bits, stage) for core in range(2)]
    moves = [relative_bits(order, r, stage == "scatter") for order in orders]
    own = lax.rem(lax.axis_index("leaf"), 1 << bits)
    core = lax.rem(lax.axis_index("group"), 2)
    return lax.bitwise_xor(own, jnp.where(core == 0, moves[0], moves[1]))


def local_kernel(bits, *refs):
    inputs, outputs = refs[:4], refs[4:8]
    loaded, (joined, sums), (in_sems,) = refs[8:12], refs[12:14], refs[14:]
    depth, rank = inputs[0].shape
    blocks = 1 << bits
    rows = rank // blocks
    parts = 2
    part = depth // parts
    copies = [
        [
            pltpu.make_async_copy(
                source.at[pl.ds(p * part, part)], target.at[pl.ds(p * part, part)], in_sems.at[p, i]
            )
            for i, (source, target) in enumerate(zip(inputs, loaded))
        ]
        for p in range(parts)
    ]
    for group in copies:
        for copy in group:
            copy.start()
    y, z, low_basis, high_basis = loaded
    dims = (((0,), (0,)), ((), ()))
    for p in range(parts):
        span = pl.ds(p * part, part)
        for copy in copies[p][:3]:
            copy.wait()
        for source, columns in ((y, pl.ds(0, rank)), (z, pl.ds(rank, 2 * rank))):
            high, low = split(source[span, :])
            joined[0, span, columns] = high
            joined[1, span, columns] = low
        term = dot3(split(low_basis[span, :]), (joined[0, span, :], joined[1, span, :]), dims)
        sums[0] = term if p == 0 else sums[0] + term
    for p in range(parts):
        copies[p][3].wait()
    sums[1] = dot3(split(high_basis[...]), (joined[0], joined[1]), dims)
    for i, chain in enumerate(("low", "high")):
        for r in range(blocks):
            start = pl.multiple_of(block_of(r, chain, bits, "scatter") * rows, rows)
            target = outputs[2 * i + (0 if r >= blocks // 2 else 1)]
            target[r % (blocks // 2)] = sums[i, pl.ds(start, rows), :]


def place(parts, chain, bits, target):
    blocks = 1 << bits
    rows = target.shape[-2] // blocks
    for r in range(blocks):
        start = pl.multiple_of(block_of(r, chain, bits, "gather") * rows, rows)
        piece = parts[r // (blocks // 2)][r % (blocks // 2)]
        if len(target.shape) == 3:
            target[:, pl.ds(start, rows), :] = piece
        else:
            target[pl.ds(start, rows), :] = piece


def solve_kernel(bits, first_ref, second_ref, update_ref, terms):
    rank = update_ref.shape[1]
    place((first_ref, second_ref), "low", bits, terms)
    couples = [split(terms[i, :, :rank]) for i in range(2)]
    for i in range(2):
        mine, other = couples[i], couples[1 - i]
        start = terms[1 - i, :, rank:] - dot3(other, split(terms[i, :, rank:]))
        update_ref[i] = start + dot3(other, split(dot3(mine, split(start))))


def total_kernel(bits, first_ref, second_ref, update_ref, total_ref, terms):
    rank = total_ref.shape[0]
    place((first_ref, second_ref), "high", bits, terms)
    total = terms[:, 2 * rank :]
    for i in range(2):
        total = total - dot3(split(terms[:, i * rank : (i + 1) * rank]), split(update_ref[i]))
    total_ref[...] = total


def middle_kernel(y_ref, z_ref, update_ref, pair_ref, halves_ref, next_ref):
    rank = y_ref.shape[1]
    middle = z_ref[...] - dot3(split(y_ref[...]), split(update_ref[0]))
    pair = middle[:, :rank]
    pair_ref[...] = pair
    halves_ref[0], halves_ref[1] = split(pair)
    next_ref[...] = middle[:, rank:]


def final_kernel(mine_ref, other_ref, halves_ref, next_ref, out_ref):
    rank = mine_ref.shape[0]
    mine = split(mine_ref[:, :rank])
    other = split(other_ref[:, :rank])
    start = other_ref[:, rank:] - dot3(other, split(mine_ref[:, rank:]))
    update = start + dot3(other, split(dot3(mine, split(start))))
    out_ref[...] = next_ref[...] - dot3((halves_ref[0], halves_ref[1]), split(update))


def run(kernel, shapes, args, scratch=(), flops=0, space=pltpu.VMEM, limit=24 << 20):
    bytes_moved = sum(a.size * 4 for a in args) + sum(4 * s.size for s in shapes)
    return pl.pallas_call(
        kernel,
        out_shape=shapes,
        in_specs=[pl.BlockSpec(memory_space=space)] * len(args),
        out_specs=[pl.BlockSpec(memory_space=pltpu.VMEM)] * len(shapes),
        scratch_shapes=list(scratch),
        compiler_params=pltpu.CompilerParams(vmem_limit_bytes=limit),
        cost_estimate=pl.CostEstimate(flops=flops, bytes_accessed=bytes_moved, transcendentals=0),
    )(*args)


def array(*shape, dtype=jnp.float32):
    return jax.ShapeDtypeStruct(shape, dtype)


def after(x, *others):
    return lax.optimization_barrier((x, *others))[0]


def body(low_solved, low_basis, upper_solved, upper_basis):
    depth, rank = low_solved.shape
    leaves = lax.axis_size("leaf")
    bits = leaves.bit_length() - 2
    blocks = 1 << bits
    rows = rank // blocks
    unit = 6 * rank * rank

    half = array(blocks // 2, rows, 3 * rank)
    low_send, low_keep, high_send, high_keep = run(
        functools.partial(local_kernel, bits),
        [half] * 4,
        [low_solved, upper_solved, low_basis, upper_basis],
        [
            pltpu.VMEM((depth, rank), jnp.float32),
            pltpu.VMEM((depth, 2 * rank), jnp.float32),
            pltpu.VMEM((depth, rank), jnp.float32),
            pltpu.VMEM((depth, rank), jnp.float32),
            pltpu.VMEM((2, depth, 3 * rank), jnp.bfloat16),
            pltpu.VMEM((2, rank, 3 * rank), jnp.float32),
            pltpu.SemaphoreType.DMA((2, 4)),
        ],
        flops=6 * unit * depth,
        space=pltpu.HBM,
        limit=(62 << 20) + (1 << 18),
    )

    def rounds(chain, send, keep):
        for t in range(bits):
            got = yield send, functools.partial(step, chain=chain, t=t, bits=bits, stage="scatter")
            half = keep.shape[0] // 2
            if t < bits - 1:
                send = keep[half:] + got[half:]
                keep = keep[:half] + got[:half]
        mine = keep[0] + got[0]
        other = yield mine, functools.partial(flip, axis="leaf", bit=bits)
        if chain == "low":
            grown = jnp.stack([mine, other])[None]
        else:
            both = [mine[:, :rank], other[:, :rank], mine[:, rank:] + other[:, rank:]]
            grown = jnp.concatenate(both, axis=1)[None]
        for t in range(bits):
            got = yield grown, functools.partial(step, chain=chain, t=t, bits=bits, stage="gather")
            if t < bits - 1:
                grown = jnp.concatenate([grown, got], axis=0)
        yield (grown, got), None

    low, high = rounds("low", low_send, low_keep), rounds("high", high_send, high_keep)
    (low_out, low_move), (high_out, high_move) = next(low), next(high)
    while low_move is not None:
        low_got, high_got = low_move(low_out), high_move(high_out)
        low_out, low_move = low.send(after(low_got, high_out))
        if low_move is not None:
            high_got = after(high_got, low_out)
        high_out, high_move = high.send(high_got)
    low_parts, high_parts = low_out, high_out

    (update,) = run(
        functools.partial(solve_kernel, bits),
        [array(2, rank, 2 * rank)],
        low_parts,
        [pltpu.VMEM((2, rank, 3 * rank), jnp.float32)],
        flops=12 * unit * rank,
    )
    (total,) = run(
        functools.partial(total_kernel, bits),
        [array(rank, 2 * rank)],
        [*high_parts, update],
        [pltpu.VMEM((rank, 4 * rank), jnp.float32)],
        flops=4 * unit * rank,
    )
    sibling = flip(total, "group", 0)
    pair_solved, halves, next_terms = run(
        middle_kernel,
        [array(depth, rank), array(2, depth, rank, dtype=jnp.bfloat16), array(depth, rank)],
        [low_solved, upper_solved, update],
        flops=2 * unit * depth,
    )
    (next_solved,) = run(
        final_kernel,
        [array(depth, rank)],
        [total, sibling, halves, next_terms],
        flops=3 * unit * rank + unit * depth,
    )
    return pair_solved, next_solved


def solution(mesh):
    spec = P(("group", "leaf"), None)
    return jax.shard_map(
        body,
        mesh=mesh,
        in_specs=(spec, spec, spec, spec),
        out_specs=(spec, spec),
        check_vma=False,
    )
```

```python
import functools

import jax
import jax.numpy as jnp
from jax import lax
from jax.experimental import pallas as pl
from jax.experimental.pallas import tpu as pltpu
from jax.sharding import PartitionSpec as P

AXES = ("leaf", "group")


def axis_order(chain, core, bits, stage):
    if stage == "gather":
        first = core if chain == "low" else 2
        return [(first + t) % bits for t in range(bits)]
    pair, rest = [core, 1 - core], list(range(2, bits))
    return pair + rest if chain == "low" else rest + pair


def relative_bits(order, r, first_is_high):
    bits = len(order)
    out = 0
    for t in range(bits):
        place = bits - 1 - t if first_is_high else t
        if (r >> place) & 1:
            out |= 1 << order[t]
    return out


def step(x, chain, t, bits, stage):
    leaves, groups = lax.axis_size("leaf"), lax.axis_size("group")
    pairs = []
    for leaf in range(leaves):
        for group in range(groups):
            bit = axis_order(chain, group % 2, bits, stage)[t]
            pairs.append((leaf * groups + group, (leaf ^ (1 << bit)) * groups + group))
    return lax.ppermute(x, AXES, pairs)


def flip(x, axis, bit):
    return lax.ppermute(x, axis, [(i, i ^ (1 << bit)) for i in range(lax.axis_size(axis))])


def split(x):
    high = x.astype(jnp.bfloat16)
    low = (x - high.astype(jnp.float32)).astype(jnp.bfloat16)
    return high, low


def dot3(left, right, dims=(((1,), (0,)), ((), ()))):
    dot = functools.partial(
        lax.dot_general, dimension_numbers=dims, preferred_element_type=jnp.float32
    )
    return dot(left[0], right[0]) + (dot(left[0], right[1]) + dot(left[1], right[0]))


def block_of(r, chain, bits, stage):
    orders = [axis_order(chain, core, bits, stage) for core in range(2)]
    moves = [relative_bits(order, r, stage == "scatter") for order in orders]
    own = lax.rem(lax.axis_index("leaf"), 1 << bits)
    core = lax.rem(lax.axis_index("group"), 2)
    return lax.bitwise_xor(own, jnp.where(core == 0, moves[0], moves[1]))


def local_kernel(bits, *refs):
    inputs, outputs = refs[:4], refs[4:8]
    loaded, (joined, sums), (in_sems,) = refs[8:12], refs[12:14], refs[14:]
    depth, rank = inputs[0].shape
    blocks = 1 << bits
    rows = rank // blocks
    parts = 2
    part = depth // parts
    copies = [
        [
            pltpu.make_async_copy(
                source.at[pl.ds(p * part, part)], target.at[pl.ds(p * part, part)], in_sems.at[p, i]
            )
            for i, (source, target) in enumerate(zip(inputs, loaded))
        ]
        for p in range(parts)
    ]
    for group in copies:
        for copy in group:
            copy.start()
    y, z, low_basis, high_basis = loaded
    dims = (((0,), (0,)), ((), ()))
    for p in range(parts):
        span = pl.ds(p * part, part)
        for copy in copies[p][:3]:
            copy.wait()
        for source, columns in ((y, pl.ds(0, rank)), (z, pl.ds(rank, 2 * rank))):
            high, low = split(source[span, :])
            joined[0, span, columns] = high
            joined[1, span, columns] = low
        term = dot3(split(low_basis[span, :]), (joined[0, span, :], joined[1, span, :]), dims)
        sums[0] = term if p == 0 else sums[0] + term
    for p in range(parts):
        copies[p][3].wait()
    sums[1] = dot3(split(high_basis[...]), (joined[0], joined[1]), dims)
    for i, chain in enumerate(("low", "high")):
        for r in range(blocks):
            start = pl.multiple_of(block_of(r, chain, bits, "scatter") * rows, rows)
            target = outputs[2 * i + (0 if r >= blocks // 2 else 1)]
            target[r % (blocks // 2)] = sums[i, pl.ds(start, rows), :]


def place(parts, chain, bits, target):
    blocks = 1 << bits
    rows = target.shape[0] // blocks
    for r in range(blocks):
        start = pl.multiple_of(block_of(r, chain, bits, "gather") * rows, rows)
        target[pl.ds(start, rows), :] = parts[r // (blocks // 2)][r % (blocks // 2)]


def solve_kernel(bits, first_ref, second_ref, update_ref, share_ref, terms):
    rank = update_ref.shape[1]
    place((first_ref, second_ref), "low", bits, terms)
    couples = [split(terms[:, 3 * i * rank : (3 * i + 1) * rank]) for i in range(2)]
    sides = [terms[:, (3 * i + 1) * rank : (3 * i + 3) * rank] for i in range(2)]
    for i in range(2):
        mine, other = couples[i], couples[1 - i]
        start = sides[1 - i] - dot3(other, split(sides[i]))
        update_ref[i] = start + dot3(other, split(dot3(mine, split(start))))
    share_ref[...] = dot3(split(terms[:, 6 * rank :]), split(update_ref[0]))


def total_kernel(bits, first_ref, second_ref, update_ref, share_ref, total_ref, terms):
    rank = total_ref.shape[0]
    place((first_ref, second_ref), "high", bits, terms)
    share = dot3(split(terms[:, :rank]), split(update_ref[1]))
    total_ref[...] = terms[:, rank:] - share_ref[...] - share


def middle_kernel(y_ref, z_ref, update_ref, pair_ref, halves_ref, next_ref):
    rank = y_ref.shape[1]
    middle = z_ref[...] - dot3(split(y_ref[...]), split(update_ref[0]))
    pair = middle[:, :rank]
    pair_ref[...] = pair
    halves_ref[0], halves_ref[1] = split(pair)
    next_ref[...] = middle[:, rank:]


def final_kernel(mine_ref, other_ref, halves_ref, next_ref, out_ref):
    rank = mine_ref.shape[0]
    mine = split(mine_ref[:, :rank])
    other = split(other_ref[:, :rank])
    start = other_ref[:, rank:] - dot3(other, split(mine_ref[:, rank:]))
    update = start + dot3(other, split(dot3(mine, split(start))))
    out_ref[...] = next_ref[...] - dot3((halves_ref[0], halves_ref[1]), split(update))


def run(kernel, shapes, args, scratch=(), flops=0, space=pltpu.VMEM, limit=24 << 20):
    bytes_moved = sum(a.size * 4 for a in args) + sum(4 * s.size for s in shapes)
    return pl.pallas_call(
        kernel,
        out_shape=shapes,
        in_specs=[pl.BlockSpec(memory_space=space)] * len(args),
        out_specs=[pl.BlockSpec(memory_space=pltpu.VMEM)] * len(shapes),
        scratch_shapes=list(scratch),
        compiler_params=pltpu.CompilerParams(vmem_limit_bytes=limit),
        cost_estimate=pl.CostEstimate(flops=flops, bytes_accessed=bytes_moved, transcendentals=0),
    )(*args)


def array(*shape, dtype=jnp.float32):
    return jax.ShapeDtypeStruct(shape, dtype)


def after(x, *others):
    return lax.optimization_barrier((x, *others))[0]


def body(low_solved, low_basis, upper_solved, upper_basis):
    depth, rank = low_solved.shape
    leaves = lax.axis_size("leaf")
    bits = leaves.bit_length() - 2
    blocks = 1 << bits
    rows = rank // blocks
    unit = 6 * rank * rank

    half = array(blocks // 2, rows, 3 * rank)
    low_send, low_keep, high_send, high_keep = run(
        functools.partial(local_kernel, bits),
        [half] * 4,
        [low_solved, upper_solved, low_basis, upper_basis],
        [
            pltpu.VMEM((depth, rank), jnp.float32),
            pltpu.VMEM((depth, 2 * rank), jnp.float32),
            pltpu.VMEM((depth, rank), jnp.float32),
            pltpu.VMEM((depth, rank), jnp.float32),
            pltpu.VMEM((2, depth, 3 * rank), jnp.bfloat16),
            pltpu.VMEM((2, rank, 3 * rank), jnp.float32),
            pltpu.SemaphoreType.DMA((2, 4)),
        ],
        flops=6 * unit * depth,
        space=pltpu.HBM,
        limit=(62 << 20) + (1 << 18),
    )

    own = {}

    def rounds(chain, send, keep):
        for t in range(bits):
            got = yield send, functools.partial(step, chain=chain, t=t, bits=bits, stage="scatter")
            half = keep.shape[0] // 2
            if t < bits - 1:
                send = keep[half:] + got[half:]
                keep = keep[:half] + got[:half]
        mine = keep[0] + got[0]
        own[chain] = mine
        other = yield mine, functools.partial(flip, axis="leaf", bit=bits)
        if chain == "low":
            both = [mine, other, own["high"][:, :rank]]
        else:
            both = [other[:, :rank], mine[:, rank:] + other[:, rank:]]
        grown = jnp.concatenate(both, axis=1)[None]
        for t in range(bits):
            got = yield grown, functools.partial(step, chain=chain, t=t, bits=bits, stage="gather")
            if t < bits - 1:
                grown = jnp.concatenate([grown, got], axis=0)
        yield (grown, got), None

    low, high = rounds("low", low_send, low_keep), rounds("high", high_send, high_keep)
    (low_out, low_move), (high_out, high_move) = next(low), next(high)
    while low_move is not None:
        low_got, high_got = low_move(low_out), high_move(high_out)
        low_out, low_move = low.send(after(low_got, high_out))
        if low_move is not None:
            high_got = after(high_got, low_out)
        high_out, high_move = high.send(high_got)
    low_parts, high_parts = low_out, high_out

    update, share = run(
        functools.partial(solve_kernel, bits),
        [array(2, rank, 2 * rank), array(rank, 2 * rank)],
        low_parts,
        [pltpu.VMEM((rank, 7 * rank), jnp.float32)],
        flops=14 * unit * rank,
    )
    (total,) = run(
        functools.partial(total_kernel, bits),
        [array(rank, 2 * rank)],
        [*high_parts, update, share],
        [pltpu.VMEM((rank, 3 * rank), jnp.float32)],
        flops=2 * unit * rank,
    )
    sibling = flip(total, "group", 0)
    pair_solved, halves, next_terms = run(
        middle_kernel,
        [array(depth, rank), array(2, depth, rank, dtype=jnp.bfloat16), array(depth, rank)],
        [low_solved, upper_solved, update],
        flops=2 * unit * depth,
    )
    (next_solved,) = run(
        final_kernel,
        [array(depth, rank)],
        [total, sibling, halves, next_terms],
        flops=3 * unit * rank + unit * depth,
    )
    return pair_solved, next_solved


def solution(mesh):
    spec = P(("group", "leaf"), None)
    return jax.shard_map(
        body,
        mesh=mesh,
        in_specs=(spec, spec, spec, spec),
        out_specs=(spec, spec),
        check_vma=False,
    )
```

```python
import functools

import jax
import jax.numpy as jnp
from jax import lax
from jax.experimental import pallas as pl
from jax.experimental.pallas import tpu as pltpu
from jax.sharding import PartitionSpec as P

AXES = ("leaf", "group")


def axis_order(chain, core, bits, stage):
    pair, rest = [core, 1 - core], list(range(2, bits))
    if stage == "scatter":
        return pair + rest if chain == "low" else rest + pair
    return [1 - core] + rest + [core] if chain == "low" else pair + rest


def relative_bits(order, r, first_is_high):
    bits = len(order)
    out = 0
    for t in range(bits):
        place = bits - 1 - t if first_is_high else t
        if (r >> place) & 1:
            out |= 1 << order[t]
    return out


def step(x, chain, t, bits, stage):
    leaves, groups = lax.axis_size("leaf"), lax.axis_size("group")
    pairs = []
    for leaf in range(leaves):
        for group in range(groups):
            bit = axis_order(chain, group % 2, bits, stage)[t]
            pairs.append((leaf * groups + group, (leaf ^ (1 << bit)) * groups + group))
    return lax.ppermute(x, AXES, pairs)


def flip(x, axis, bit):
    return lax.ppermute(x, axis, [(i, i ^ (1 << bit)) for i in range(lax.axis_size(axis))])


def split(x):
    high = x.astype(jnp.bfloat16)
    low = (x - high.astype(jnp.float32)).astype(jnp.bfloat16)
    return high, low


def dot3(left, right, dims=(((1,), (0,)), ((), ()))):
    dot = functools.partial(
        lax.dot_general, dimension_numbers=dims, preferred_element_type=jnp.float32
    )
    return dot(left[0], right[0]) + (dot(left[0], right[1]) + dot(left[1], right[0]))


def block_of(r, chain, bits, stage):
    orders = [axis_order(chain, core, bits, stage) for core in range(2)]
    moves = [relative_bits(order, r, stage == "scatter") for order in orders]
    own = lax.rem(lax.axis_index("leaf"), 1 << bits)
    core = lax.rem(lax.axis_index("group"), 2)
    return lax.bitwise_xor(own, jnp.where(core == 0, moves[0], moves[1]))


def local_kernel(bits, *refs):
    inputs, outputs = refs[:4], refs[4:8]
    loaded, (joined, sums), (in_sems,) = refs[8:12], refs[12:14], refs[14:]
    depth, rank = inputs[0].shape
    blocks = 1 << bits
    rows = rank // blocks
    parts = 2
    part = depth // parts
    copies = [
        [
            pltpu.make_async_copy(
                source.at[pl.ds(p * part, part)], target.at[pl.ds(p * part, part)], in_sems.at[p, i]
            )
            for i, (source, target) in enumerate(zip(inputs, loaded))
        ]
        for p in range(parts)
    ]
    for group in copies:
        for copy in group:
            copy.start()
    y, z, low_basis, high_basis = loaded
    dims = (((0,), (0,)), ((), ()))
    for p in range(parts):
        span = pl.ds(p * part, part)
        for copy in copies[p][:3]:
            copy.wait()
        for source, columns in ((y, pl.ds(0, rank)), (z, pl.ds(rank, 2 * rank))):
            high, low = split(source[span, :])
            joined[0, span, columns] = high
            joined[1, span, columns] = low
        term = dot3(split(low_basis[span, :]), (joined[0, span, :], joined[1, span, :]), dims)
        sums[0] = term if p == 0 else sums[0] + term
    for p in range(parts):
        copies[p][3].wait()
    sums[1] = dot3(split(high_basis[...]), (joined[0], joined[1]), dims)
    for i, chain in enumerate(("low", "high")):
        for r in range(blocks):
            start = pl.multiple_of(block_of(r, chain, bits, "scatter") * rows, rows)
            target = outputs[2 * i + (0 if r >= blocks // 2 else 1)]
            target[r % (blocks // 2)] = sums[i, pl.ds(start, rows), :]


def place(parts, chain, bits, target):
    blocks = 1 << bits
    rows = target.shape[-2] // blocks
    for r in range(blocks):
        start = pl.multiple_of(block_of(r, chain, bits, "gather") * rows, rows)
        piece = parts[r // (blocks // 2)][r % (blocks // 2)]
        if len(target.shape) == 3:
            target[:, pl.ds(start, rows), :] = piece
        else:
            target[pl.ds(start, rows), :] = piece


def solve_kernel(bits, first_ref, second_ref, update_ref, terms):
    rank = update_ref.shape[1]
    place((first_ref, second_ref), "low", bits, terms)
    couples = [split(terms[i, :, :rank]) for i in range(2)]
    for i in range(2):
        mine, other = couples[i], couples[1 - i]
        start = terms[1 - i, :, rank:] - dot3(other, split(terms[i, :, rank:]))
        update_ref[i] = start + dot3(other, split(dot3(mine, split(start))))


def total_kernel(bits, first_ref, second_ref, update_ref, total_ref, terms):
    rank = total_ref.shape[0]
    place((first_ref, second_ref), "high", bits, terms)
    total = terms[:, 2 * rank :]
    for i in range(2):
        total = total - dot3(split(terms[:, i * rank : (i + 1) * rank]), split(update_ref[i]))
    total_ref[...] = total


def middle_kernel(y_ref, z_ref, update_ref, pair_ref, halves_ref, next_ref):
    rank = y_ref.shape[1]
    middle = z_ref[...] - dot3(split(y_ref[...]), split(update_ref[0]))
    pair = middle[:, :rank]
    pair_ref[...] = pair
    halves_ref[0], halves_ref[1] = split(pair)
    next_ref[...] = middle[:, rank:]


def final_kernel(mine_ref, other_ref, halves_ref, next_ref, out_ref):
    rank = mine_ref.shape[0]
    mine = split(mine_ref[:, :rank])
    other = split(other_ref[:, :rank])
    start = other_ref[:, rank:] - dot3(other, split(mine_ref[:, rank:]))
    update = start + dot3(other, split(dot3(mine, split(start))))
    out_ref[...] = next_ref[...] - dot3((halves_ref[0], halves_ref[1]), split(update))


def run(kernel, shapes, args, scratch=(), flops=0, space=pltpu.VMEM, limit=24 << 20):
    bytes_moved = sum(a.size * 4 for a in args) + sum(4 * s.size for s in shapes)
    return pl.pallas_call(
        kernel,
        out_shape=shapes,
        in_specs=[pl.BlockSpec(memory_space=space)] * len(args),
        out_specs=[pl.BlockSpec(memory_space=pltpu.VMEM)] * len(shapes),
        scratch_shapes=list(scratch),
        compiler_params=pltpu.CompilerParams(vmem_limit_bytes=limit),
        cost_estimate=pl.CostEstimate(flops=flops, bytes_accessed=bytes_moved, transcendentals=0),
    )(*args)


def array(*shape, dtype=jnp.float32):
    return jax.ShapeDtypeStruct(shape, dtype)


def after(x, *others):
    return lax.optimization_barrier((x, *others))[0]


def body(low_solved, low_basis, upper_solved, upper_basis):
    depth, rank = low_solved.shape
    leaves = lax.axis_size("leaf")
    bits = leaves.bit_length() - 2
    blocks = 1 << bits
    rows = rank // blocks
    unit = 6 * rank * rank

    half = array(blocks // 2, rows, 3 * rank)
    low_send, low_keep, high_send, high_keep = run(
        functools.partial(local_kernel, bits),
        [half] * 4,
        [
            pltpu.with_memory_space_constraint(x, pltpu.HBM)
            for x in (low_solved, upper_solved, low_basis, upper_basis)
        ],
        [
            pltpu.VMEM((depth, rank), jnp.float32),
            pltpu.VMEM((depth, 2 * rank), jnp.float32),
            pltpu.VMEM((depth, rank), jnp.float32),
            pltpu.VMEM((depth, rank), jnp.float32),
            pltpu.VMEM((2, depth, 3 * rank), jnp.bfloat16),
            pltpu.VMEM((2, rank, 3 * rank), jnp.float32),
            pltpu.SemaphoreType.DMA((2, 4)),
        ],
        flops=6 * unit * depth,
        space=pltpu.HBM,
    )

    def rounds(chain, send, keep):
        for t in range(bits):
            got = yield send, functools.partial(step, chain=chain, t=t, bits=bits, stage="scatter")
            half = keep.shape[0] // 2
            if t < bits - 1:
                send = keep[half:] + got[half:]
                keep = keep[:half] + got[:half]
        mine = keep[0] + got[0]
        other = yield mine, functools.partial(flip, axis="leaf", bit=bits)
        if chain == "low":
            grown = jnp.stack([mine, other])[None]
        else:
            both = [mine[:, :rank], other[:, :rank], mine[:, rank:] + other[:, rank:]]
            grown = jnp.concatenate(both, axis=1)[None]
        for t in range(bits):
            got = yield grown, functools.partial(step, chain=chain, t=t, bits=bits, stage="gather")
            if t < bits - 1:
                grown = jnp.concatenate([grown, got], axis=0)
        yield (grown, got), None

    low, high = rounds("low", low_send, low_keep), rounds("high", high_send, high_keep)
    (low_out, low_move), (high_out, high_move) = next(low), next(high)
    while low_move is not None:
        low_got, high_got = low_move(low_out), high_move(high_out)
        low_out, low_move = low.send(after(low_got, high_out))
        if low_move is not None:
            high_got = after(high_got, low_out)
        high_out, high_move = high.send(high_got)
    low_parts, high_parts = low_out, high_out

    (update,) = run(
        functools.partial(solve_kernel, bits),
        [array(2, rank, 2 * rank)],
        low_parts,
        [pltpu.VMEM((2, rank, 3 * rank), jnp.float32)],
        flops=12 * unit * rank,
    )
    (total,) = run(
        functools.partial(total_kernel, bits),
        [array(rank, 2 * rank)],
        [*high_parts, update],
        [pltpu.VMEM((rank, 4 * rank), jnp.float32)],
        flops=4 * unit * rank,
    )
    sibling = flip(total, "group", 0)
    pair_solved, halves, next_terms = run(
        middle_kernel,
        [array(depth, rank), array(2, depth, rank, dtype=jnp.bfloat16), array(depth, rank)],
        [low_solved, upper_solved, update],
        flops=2 * unit * depth,
    )
    (next_solved,) = run(
        final_kernel,
        [array(depth, rank)],
        [total, sibling, halves, next_terms],
        flops=3 * unit * rank + unit * depth,
    )
    return pair_solved, next_solved


def solution(mesh):
    spec = P(("group", "leaf"), None)
    return jax.shard_map(
        body,
        mesh=mesh,
        in_specs=(spec, spec, spec, spec),
        out_specs=(spec, spec),
        check_vma=False,
    )
```

```python
import functools

import jax
import jax.numpy as jnp
from jax import lax
from jax.experimental import pallas as pl
from jax.experimental.pallas import tpu as pltpu
from jax.sharding import PartitionSpec as P

AXES = ("leaf", "group")


def axis_order(chain, core, bits, stage):
    pair, rest = [core, 1 - core], list(range(2, bits))
    if stage == "scatter":
        return pair + rest if chain == "low" else rest + pair
    return [1 - core] + rest + [core] if chain == "low" else pair + rest


def relative_bits(order, r, first_is_high):
    bits = len(order)
    out = 0
    for t in range(bits):
        place = bits - 1 - t if first_is_high else t
        if (r >> place) & 1:
            out |= 1 << order[t]
    return out


def step(x, chain, t, bits, stage):
    leaves, groups = lax.axis_size("leaf"), lax.axis_size("group")
    pairs = []
    for leaf in range(leaves):
        for group in range(groups):
            bit = axis_order(chain, group % 2, bits, stage)[t]
            pairs.append((leaf * groups + group, (leaf ^ (1 << bit)) * groups + group))
    return lax.ppermute(x, AXES, pairs)


def flip(x, axis, bit):
    return lax.ppermute(x, axis, [(i, i ^ (1 << bit)) for i in range(lax.axis_size(axis))])


def split(x):
    high = x.astype(jnp.bfloat16)
    low = (x - high.astype(jnp.float32)).astype(jnp.bfloat16)
    return high, low


def dot3(left, right, dims=(((1,), (0,)), ((), ()))):
    dot = functools.partial(
        lax.dot_general, dimension_numbers=dims, preferred_element_type=jnp.float32
    )
    return dot(left[0], right[0]) + (dot(left[0], right[1]) + dot(left[1], right[0]))


def block_of(r, chain, bits, stage):
    orders = [axis_order(chain, core, bits, stage) for core in range(2)]
    moves = [relative_bits(order, r, stage == "scatter") for order in orders]
    own = lax.rem(lax.axis_index("leaf"), 1 << bits)
    core = lax.rem(lax.axis_index("group"), 2)
    return lax.bitwise_xor(own, jnp.where(core == 0, moves[0], moves[1]))


def hand_out(sums, chain, bits, send_ref, keep_ref):
    blocks = 1 << bits
    rows = sums.shape[0] // blocks
    for r in range(blocks):
        start = pl.multiple_of(block_of(r, chain, bits, "scatter") * rows, rows)
        target = send_ref if r >= blocks // 2 else keep_ref
        target[r % (blocks // 2)] = sums[pl.ds(start, rows), :]


def low_kernel(bits, *refs):
    inputs, (send_ref, keep_ref, joined) = refs[:3], refs[3:6]
    loaded, (sums, sems) = refs[6:9], refs[9:]
    depth, rank = inputs[0].shape
    parts = sems.shape[0]
    part = depth // parts
    copies = [
        [
            pltpu.make_async_copy(
                source.at[pl.ds(p * part, part)], target.at[pl.ds(p * part, part)], sems.at[p, i]
            )
            for i, (source, target) in enumerate(zip(inputs, loaded))
        ]
        for p in range(parts)
    ]
    for group in copies:
        for copy in group:
            copy.start()
    y, z, basis = loaded
    dims = (((0,), (0,)), ((), ()))
    for p in range(parts):
        span = pl.ds(p * part, part)
        for copy in copies[p]:
            copy.wait()
        for source, columns in ((y, pl.ds(0, rank)), (z, pl.ds(rank, 2 * rank))):
            high, low = split(source[span, :])
            joined[0, span, columns] = high
            joined[1, span, columns] = low
        term = dot3(split(basis[span, :]), (joined[0, span, :], joined[1, span, :]), dims)
        sums[...] = term if p == 0 else sums[...] + term
    hand_out(sums, "low", bits, send_ref, keep_ref)


def high_kernel(bits, basis_ref, joined, send_ref, keep_ref, sums):
    dims = (((0,), (0,)), ((), ()))
    sums[...] = dot3(split(basis_ref[...]), (joined[0], joined[1]), dims)
    hand_out(sums, "high", bits, send_ref, keep_ref)


def place(parts, chain, bits, target):
    blocks = 1 << bits
    rows = target.shape[-2] // blocks
    for r in range(blocks):
        start = pl.multiple_of(block_of(r, chain, bits, "gather") * rows, rows)
        piece = parts[r // (blocks // 2)][r % (blocks // 2)]
        if len(target.shape) == 3:
            target[:, pl.ds(start, rows), :] = piece
        else:
            target[pl.ds(start, rows), :] = piece


def solve_kernel(bits, first_ref, second_ref, update_ref, terms):
    rank = update_ref.shape[1]
    place((first_ref, second_ref), "low", bits, terms)
    couples = [split(terms[i, :, :rank]) for i in range(2)]
    for i in range(2):
        mine, other = couples[i], couples[1 - i]
        start = terms[1 - i, :, rank:] - dot3(other, split(terms[i, :, rank:]))
        update_ref[i] = start + dot3(other, split(dot3(mine, split(start))))


def total_kernel(bits, first_ref, second_ref, update_ref, total_ref, terms):
    rank = total_ref.shape[0]
    place((first_ref, second_ref), "high", bits, terms)
    total = terms[:, 2 * rank :]
    for i in range(2):
        total = total - dot3(split(terms[:, i * rank : (i + 1) * rank]), split(update_ref[i]))
    total_ref[...] = total


def middle_kernel(y_ref, z_ref, update_ref, pair_ref, halves_ref, next_ref):
    rank = y_ref.shape[1]
    middle = z_ref[...] - dot3(split(y_ref[...]), split(update_ref[0]))
    pair = middle[:, :rank]
    pair_ref[...] = pair
    halves_ref[0], halves_ref[1] = split(pair)
    next_ref[...] = middle[:, rank:]


def final_kernel(mine_ref, other_ref, halves_ref, next_ref, out_ref):
    rank = mine_ref.shape[0]
    mine = split(mine_ref[:, :rank])
    other = split(other_ref[:, :rank])
    start = other_ref[:, rank:] - dot3(other, split(mine_ref[:, rank:]))
    update = start + dot3(other, split(dot3(mine, split(start))))
    out_ref[...] = next_ref[...] - dot3((halves_ref[0], halves_ref[1]), split(update))


def run(kernel, shapes, args, scratch=(), flops=0, space=pltpu.VMEM, limit=24 << 20):
    bytes_moved = sum(a.size * 4 for a in args) + sum(4 * s.size for s in shapes)
    return pl.pallas_call(
        kernel,
        out_shape=shapes,
        in_specs=[pl.BlockSpec(memory_space=space)] * len(args),
        out_specs=[pl.BlockSpec(memory_space=pltpu.VMEM)] * len(shapes),
        scratch_shapes=list(scratch),
        compiler_params=pltpu.CompilerParams(vmem_limit_bytes=limit),
        cost_estimate=pl.CostEstimate(flops=flops, bytes_accessed=bytes_moved, transcendentals=0),
    )(*args)


def array(*shape, dtype=jnp.float32):
    return jax.ShapeDtypeStruct(shape, dtype)


def after(x, *others):
    return lax.optimization_barrier((x, *others))[0]


def body(low_solved, low_basis, upper_solved, upper_basis):
    depth, rank = low_solved.shape
    leaves = lax.axis_size("leaf")
    bits = leaves.bit_length() - 2
    blocks = 1 << bits
    rows = rank // blocks
    unit = 6 * rank * rank

    half = array(blocks // 2, rows, 3 * rank)
    low_send, low_keep, joined = run(
        functools.partial(low_kernel, bits),
        [half, half, array(2, depth, 3 * rank, dtype=jnp.bfloat16)],
        [
            pltpu.with_memory_space_constraint(x, pltpu.HBM)
            for x in (low_solved, upper_solved, low_basis)
        ],
        [
            pltpu.VMEM((depth, rank), jnp.float32),
            pltpu.VMEM((depth, 2 * rank), jnp.float32),
            pltpu.VMEM((depth, rank), jnp.float32),
            pltpu.VMEM((rank, 3 * rank), jnp.float32),
            pltpu.SemaphoreType.DMA((2, 3)),
        ],
        flops=3 * unit * depth,
        space=pltpu.HBM,
    )
    high_send, high_keep = run(
        functools.partial(high_kernel, bits),
        [half, half],
        [upper_basis, joined],
        [pltpu.VMEM((rank, 3 * rank), jnp.float32)],
        flops=3 * unit * depth,
    )

    def rounds(chain, send, keep):
        for t in range(bits):
            got = yield send, functools.partial(step, chain=chain, t=t, bits=bits, stage="scatter")
            half = keep.shape[0] // 2
            if t < bits - 1:
                send = keep[half:] + got[half:]
                keep = keep[:half] + got[:half]
        mine = keep[0] + got[0]
        other = yield mine, functools.partial(flip, axis="leaf", bit=bits)
        if chain == "low":
            grown = jnp.stack([mine, other])[None]
        else:
            both = [mine[:, :rank], other[:, :rank], mine[:, rank:] + other[:, rank:]]
            grown = jnp.concatenate(both, axis=1)[None]
        for t in range(bits):
            got = yield grown, functools.partial(step, chain=chain, t=t, bits=bits, stage="gather")
            if t < bits - 1:
                grown = jnp.concatenate([grown, got], axis=0)
        yield (grown, got), None

    low, high = rounds("low", low_send, low_keep), rounds("high", high_send, high_keep)
    (low_out, low_move), (high_out, high_move) = next(low), next(high)
    for t in range(2 * bits + 1):
        low_got, high_got = low_move(low_out), high_move(high_out)
        if bits < t < 2 * bits:
            high_out, high_move = high.send(high_got)
            low_out, low_move = low.send(after(low_got, high_out))
        else:
            low_out, low_move = low.send(after(low_got, high_out))
            if low_move is not None:
                high_got = after(high_got, low_out)
            high_out, high_move = high.send(high_got)
    low_parts, high_parts = low_out, high_out

    (update,) = run(
        functools.partial(solve_kernel, bits),
        [array(2, rank, 2 * rank)],
        low_parts,
        [pltpu.VMEM((2, rank, 3 * rank), jnp.float32)],
        flops=12 * unit * rank,
    )
    (total,) = run(
        functools.partial(total_kernel, bits),
        [array(rank, 2 * rank)],
        [*high_parts, update],
        [pltpu.VMEM((rank, 4 * rank), jnp.float32)],
        flops=4 * unit * rank,
    )
    sibling = flip(total, "group", 0)
    pair_solved, halves, next_terms = run(
        middle_kernel,
        [array(depth, rank), array(2, depth, rank, dtype=jnp.bfloat16), array(depth, rank)],
        [low_solved, upper_solved, update],
        flops=2 * unit * depth,
    )
    (next_solved,) = run(
        final_kernel,
        [array(depth, rank)],
        [total, sibling, halves, next_terms],
        flops=3 * unit * rank + unit * depth,
    )
    return pair_solved, next_solved


def solution(mesh):
    spec = P(("group", "leaf"), None)
    return jax.shard_map(
        body,
        mesh=mesh,
        in_specs=(spec, spec, spec, spec),
        out_specs=(spec, spec),
        check_vma=False,
    )
```

```python
import functools

import jax
import jax.numpy as jnp
from jax import lax
from jax.experimental import pallas as pl
from jax.experimental.pallas import tpu as pltpu
from jax.sharding import PartitionSpec as P

AXES = ("leaf", "group")


def axis_order(chain, core, bits, stage):
    pair, rest = [core, 1 - core], list(range(2, bits))
    if stage == "scatter":
        return pair + rest if chain == "low" else rest + pair
    return {"own": pair + rest, "other": rest + pair[::-1], "high": rest + pair}[chain]


def relative_bits(order, r, first_is_high):
    bits = len(order)
    out = 0
    for t in range(bits):
        place = bits - 1 - t if first_is_high else t
        if (r >> place) & 1:
            out |= 1 << order[t]
    return out


def step(x, chain, t, bits, stage):
    leaves, groups = lax.axis_size("leaf"), lax.axis_size("group")
    pairs = []
    for leaf in range(leaves):
        for group in range(groups):
            bit = axis_order(chain, group % 2, bits, stage)[t]
            pairs.append((leaf * groups + group, (leaf ^ (1 << bit)) * groups + group))
    return lax.ppermute(x, AXES, pairs)


def flip(x, axis, bit):
    return lax.ppermute(x, axis, [(i, i ^ (1 << bit)) for i in range(lax.axis_size(axis))])


def split(x):
    high = x.astype(jnp.bfloat16)
    low = (x - high.astype(jnp.float32)).astype(jnp.bfloat16)
    return high, low


def dot3(left, right, dims=(((1,), (0,)), ((), ()))):
    dot = functools.partial(
        lax.dot_general, dimension_numbers=dims, preferred_element_type=jnp.float32
    )
    return dot(left[0], right[0]) + (dot(left[0], right[1]) + dot(left[1], right[0]))


def block_of(r, chain, bits, stage):
    orders = [axis_order(chain, core, bits, stage) for core in range(2)]
    moves = [relative_bits(order, r, stage == "scatter") for order in orders]
    own = lax.rem(lax.axis_index("leaf"), 1 << bits)
    core = lax.rem(lax.axis_index("group"), 2)
    return lax.bitwise_xor(own, jnp.where(core == 0, moves[0], moves[1]))


def hand_out(sums, chain, bits, send_ref, keep_ref):
    blocks = 1 << bits
    rows = sums.shape[0] // blocks
    for r in range(blocks):
        start = pl.multiple_of(block_of(r, chain, bits, "scatter") * rows, rows)
        target = send_ref if r >= blocks // 2 else keep_ref
        target[r % (blocks // 2)] = sums[pl.ds(start, rows), :]


def low_kernel(bits, *refs):
    inputs, (send_ref, keep_ref, joined) = refs[:3], refs[3:6]
    loaded, (sums, sems) = refs[6:9], refs[9:]
    depth, rank = inputs[0].shape
    parts = sems.shape[0]
    part = depth // parts
    copies = [
        [
            pltpu.make_async_copy(
                source.at[pl.ds(p * part, part)], target.at[pl.ds(p * part, part)], sems.at[p, i]
            )
            for i, (source, target) in enumerate(zip(inputs, loaded))
        ]
        for p in range(parts)
    ]
    for group in copies:
        for copy in group:
            copy.start()
    y, z, basis = loaded
    dims = (((0,), (0,)), ((), ()))
    for p in range(parts):
        span = pl.ds(p * part, part)
        for copy in copies[p]:
            copy.wait()
        for source, columns in ((y, pl.ds(0, rank)), (z, pl.ds(rank, 2 * rank))):
            high, low = split(source[span, :])
            joined[0, span, columns] = high
            joined[1, span, columns] = low
        term = dot3(split(basis[span, :]), (joined[0, span, :], joined[1, span, :]), dims)
        sums[...] = term if p == 0 else sums[...] + term
    hand_out(sums, "low", bits, send_ref, keep_ref)


def high_kernel(bits, basis_ref, joined, send_ref, keep_ref, sums):
    dims = (((0,), (0,)), ((), ()))
    sums[...] = dot3(split(basis_ref[...]), (joined[0], joined[1]), dims)
    hand_out(sums, "high", bits, send_ref, keep_ref)


def place(parts, chain, bits, target):
    blocks = 1 << bits
    rows = target.shape[0] // blocks
    for r in range(blocks):
        start = pl.multiple_of(block_of(r, chain, bits, "gather") * rows, rows)
        target[pl.ds(start, rows), :] = parts[r // (blocks // 2)][r % (blocks // 2)]


def solve_kernel(bits, own_low, own_high, other_low, other_high, update_ref, own, other):
    rank = update_ref.shape[1]
    place((own_low, own_high), "own", bits, own)
    place((other_low, other_high), "other", bits, other)
    terms = (own, other)
    couples = [split(x[:, :rank]) for x in terms]
    for i in range(2):
        mine, far = couples[i], couples[1 - i]
        start = terms[1 - i][:, rank:] - dot3(far, split(terms[i][:, rank:]))
        update_ref[i] = start + dot3(far, split(dot3(mine, split(start))))


def total_kernel(bits, first_ref, second_ref, update_ref, total_ref, terms):
    rank = total_ref.shape[0]
    place((first_ref, second_ref), "high", bits, terms)
    total = terms[:, 2 * rank :]
    for i in range(2):
        total = total - dot3(split(terms[:, i * rank : (i + 1) * rank]), split(update_ref[i]))
    total_ref[...] = total


def middle_kernel(y_ref, z_ref, update_ref, pair_ref, halves_ref, next_ref):
    rank = y_ref.shape[1]
    middle = z_ref[...] - dot3(split(y_ref[...]), split(update_ref[0]))
    pair = middle[:, :rank]
    pair_ref[...] = pair
    halves_ref[0], halves_ref[1] = split(pair)
    next_ref[...] = middle[:, rank:]


def final_kernel(mine_ref, other_ref, halves_ref, next_ref, out_ref):
    rank = mine_ref.shape[0]
    mine = split(mine_ref[:, :rank])
    other = split(other_ref[:, :rank])
    start = other_ref[:, rank:] - dot3(other, split(mine_ref[:, rank:]))
    update = start + dot3(other, split(dot3(mine, split(start))))
    out_ref[...] = next_ref[...] - dot3((halves_ref[0], halves_ref[1]), split(update))


def run(kernel, shapes, args, scratch=(), flops=0, space=pltpu.VMEM, limit=24 << 20):
    bytes_moved = sum(a.size * 4 for a in args) + sum(4 * s.size for s in shapes)
    return pl.pallas_call(
        kernel,
        out_shape=shapes,
        in_specs=[pl.BlockSpec(memory_space=space)] * len(args),
        out_specs=[pl.BlockSpec(memory_space=pltpu.VMEM)] * len(shapes),
        scratch_shapes=list(scratch),
        compiler_params=pltpu.CompilerParams(vmem_limit_bytes=limit),
        cost_estimate=pl.CostEstimate(flops=flops, bytes_accessed=bytes_moved, transcendentals=0),
    )(*args)


def array(*shape, dtype=jnp.float32):
    return jax.ShapeDtypeStruct(shape, dtype)


def after(x, *others):
    return lax.optimization_barrier((x, *others))[0]


def body(low_solved, low_basis, upper_solved, upper_basis):
    depth, rank = low_solved.shape
    leaves = lax.axis_size("leaf")
    bits = leaves.bit_length() - 2
    blocks = 1 << bits
    rows = rank // blocks
    unit = 6 * rank * rank

    half = array(blocks // 2, rows, 3 * rank)
    low_send, low_keep, joined = run(
        functools.partial(low_kernel, bits),
        [half, half, array(2, depth, 3 * rank, dtype=jnp.bfloat16)],
        [
            pltpu.with_memory_space_constraint(x, pltpu.HBM)
            for x in (low_solved, upper_solved, low_basis)
        ],
        [
            pltpu.VMEM((depth, rank), jnp.float32),
            pltpu.VMEM((depth, 2 * rank), jnp.float32),
            pltpu.VMEM((depth, rank), jnp.float32),
            pltpu.VMEM((rank, 3 * rank), jnp.float32),
            pltpu.SemaphoreType.DMA((2, 3)),
        ],
        flops=3 * unit * depth,
        space=pltpu.HBM,
    )
    high_send, high_keep = run(
        functools.partial(high_kernel, bits),
        [half, half],
        [upper_basis, joined],
        [pltpu.VMEM((rank, 3 * rank), jnp.float32)],
        flops=3 * unit * depth,
    )

    def merge(keep, got):
        half = keep.shape[0] // 2
        if half == 0:
            return keep[0] + got[0], None
        return keep[half:] + got[half:], keep[:half] + got[:half]

    def grow(x, got):
        return jnp.concatenate([x, got], axis=0)

    for t in range(bits):
        low_got = step(low_send, "low", t, bits, "scatter")
        high_got = step(high_send, "high", t, bits, "scatter")
        low_send, low_keep = merge(low_keep, after(low_got, high_send))
        high_send, high_keep = merge(high_keep, after(high_got, low_send))
    low_mine, high_mine = low_send, high_send
    low_other, high_other = flip(low_mine, "leaf", bits), flip(high_mine, "leaf", bits)

    other, own = after(low_other, high_mine)[None], low_mine[None]
    own = grow(own, after(step(own, "own", 0, bits, "gather"), other))
    high_other = after(high_other, own)
    both = [high_mine[:, :rank], high_other[:, :rank], high_mine[:, rank:] + high_other[:, rank:]]
    high = jnp.concatenate(both, axis=1)[None]
    for t in range(bits - 1):
        other_got = step(other, "other", t, bits, "gather")
        own_got = step(own, "own", t + 1, bits, "gather")
        high_got = step(high, "high", t, bits, "gather")
        other = grow(other, after(other_got, high))
        own_got = after(own_got, other)
        if t < bits - 2:
            own = grow(own, own_got)
        high = grow(high, after(high_got, own_got))
    low_parts = [own, own_got, other, step(other, "other", bits - 1, bits, "gather")]
    high_parts = [high, step(high, "high", bits - 1, bits, "gather")]

    (update,) = run(
        functools.partial(solve_kernel, bits),
        [array(2, rank, 2 * rank)],
        low_parts,
        [pltpu.VMEM((rank, 3 * rank), jnp.float32)] * 2,
        flops=12 * unit * rank,
    )
    (total,) = run(
        functools.partial(total_kernel, bits),
        [array(rank, 2 * rank)],
        [*high_parts, update],
        [pltpu.VMEM((rank, 4 * rank), jnp.float32)],
        flops=4 * unit * rank,
    )
    sibling = flip(total, "group", 0)
    pair_solved, halves, next_terms = run(
        middle_kernel,
        [array(depth, rank), array(2, depth, rank, dtype=jnp.bfloat16), array(depth, rank)],
        [low_solved, upper_solved, update],
        flops=2 * unit * depth,
    )
    (next_solved,) = run(
        final_kernel,
        [array(depth, rank)],
        [total, sibling, halves, next_terms],
        flops=3 * unit * rank + unit * depth,
    )
    return pair_solved, next_solved


def solution(mesh):
    spec = P(("group", "leaf"), None)
    return jax.shard_map(
        body,
        mesh=mesh,
        in_specs=(spec, spec, spec, spec),
        out_specs=(spec, spec),
        check_vma=False,
    )
```

```python
import functools

import jax
import jax.numpy as jnp
from jax import lax
from jax.experimental import pallas as pl
from jax.experimental.pallas import tpu as pltpu
from jax.sharding import PartitionSpec as P

AXES = ("leaf", "group")


def axis_order(chain, core, bits, stage):
    pair, rest = [core, 1 - core], list(range(2, bits))
    if stage == "scatter":
        return pair + rest if chain == "low" else rest + pair
    return {"own": pair + rest, "other": rest + pair[::-1], "high": rest + pair}[chain]


def relative_bits(order, r, first_is_high):
    bits = len(order)
    out = 0
    for t in range(bits):
        place = bits - 1 - t if first_is_high else t
        if (r >> place) & 1:
            out |= 1 << order[t]
    return out


def step(x, chain, t, bits, stage):
    leaves, groups = lax.axis_size("leaf"), lax.axis_size("group")
    pairs = []
    for leaf in range(leaves):
        for group in range(groups):
            bit = axis_order(chain, group % 2, bits, stage)[t]
            pairs.append((leaf * groups + group, (leaf ^ (1 << bit)) * groups + group))
    with jax.named_scope(f"{chain}_{stage}_{t}"):
        return lax.ppermute(x, AXES, pairs)


def flip(x, axis, bit):
    return lax.ppermute(x, axis, [(i, i ^ (1 << bit)) for i in range(lax.axis_size(axis))])


def split(x):
    high = x.astype(jnp.bfloat16)
    low = (x - high.astype(jnp.float32)).astype(jnp.bfloat16)
    return high, low


def dot3(left, right, dims=(((1,), (0,)), ((), ()))):
    dot = functools.partial(
        lax.dot_general, dimension_numbers=dims, preferred_element_type=jnp.float32
    )
    return dot(left[0], right[0]) + (dot(left[0], right[1]) + dot(left[1], right[0]))


def block_of(r, chain, bits, stage):
    orders = [axis_order(chain, core, bits, stage) for core in range(2)]
    moves = [relative_bits(order, r, stage == "scatter") for order in orders]
    own = lax.rem(lax.axis_index("leaf"), 1 << bits)
    core = lax.rem(lax.axis_index("group"), 2)
    return lax.bitwise_xor(own, jnp.where(core == 0, moves[0], moves[1]))


def hand_out(sums, chain, bits, send_ref, keep_ref):
    blocks = 1 << bits
    rows = sums.shape[0] // blocks
    for r in range(blocks):
        start = pl.multiple_of(block_of(r, chain, bits, "scatter") * rows, rows)
        target = send_ref if r >= blocks // 2 else keep_ref
        target[r % (blocks // 2)] = sums[pl.ds(start, rows), :]


def low_kernel(bits, *refs):
    inputs, (send_ref, keep_ref, joined) = refs[:3], refs[3:6]
    loaded, (sums, sems) = refs[6:9], refs[9:]
    depth, rank = inputs[0].shape
    parts = sems.shape[0]
    part = depth // parts
    copies = [
        [
            pltpu.make_async_copy(
                source.at[pl.ds(p * part, part)], target.at[pl.ds(p * part, part)], sems.at[p, i]
            )
            for i, (source, target) in enumerate(zip(inputs, loaded))
        ]
        for p in range(parts)
    ]
    for group in copies:
        for copy in group:
            copy.start()
    y, z, basis = loaded
    dims = (((0,), (0,)), ((), ()))
    for p in range(parts):
        span = pl.ds(p * part, part)
        for copy in copies[p]:
            copy.wait()
        for source, columns in ((y, pl.ds(0, rank)), (z, pl.ds(rank, 2 * rank))):
            high, low = split(source[span, :])
            joined[0, span, columns] = high
            joined[1, span, columns] = low
        term = dot3(split(basis[span, :]), (joined[0, span, :], joined[1, span, :]), dims)
        sums[...] = term if p == 0 else sums[...] + term
    hand_out(sums, "low", bits, send_ref, keep_ref)


def high_kernel(bits, basis_ref, joined, send_ref, keep_ref, sums):
    dims = (((0,), (0,)), ((), ()))
    sums[...] = dot3(split(basis_ref[...]), (joined[0], joined[1]), dims)
    hand_out(sums, "high", bits, send_ref, keep_ref)


def place(parts, chain, bits, target):
    blocks = 1 << bits
    rows = target.shape[0] // blocks
    for r in range(blocks):
        start = pl.multiple_of(block_of(r, chain, bits, "gather") * rows, rows)
        target[pl.ds(start, rows), :] = parts[r // (blocks // 2)][r % (blocks // 2)]


def solve_kernel(bits, own_low, own_high, other_low, other_high, update_ref, own, other):
    rank = update_ref.shape[1]
    place((own_low, own_high), "own", bits, own)
    place((other_low, other_high), "other", bits, other)
    terms = (own, other)
    couples = [split(x[:, :rank]) for x in terms]
    for i in range(2):
        mine, far = couples[i], couples[1 - i]
        start = terms[1 - i][:, rank:] - dot3(far, split(terms[i][:, rank:]))
        update_ref[i] = start + dot3(far, split(dot3(mine, split(start))))


def total_kernel(bits, first_ref, second_ref, update_ref, total_ref, terms):
    rank = total_ref.shape[0]
    place((first_ref, second_ref), "high", bits, terms)
    total = terms[:, 2 * rank :]
    for i in range(2):
        total = total - dot3(split(terms[:, i * rank : (i + 1) * rank]), split(update_ref[i]))
    total_ref[...] = total


def middle_kernel(y_ref, z_ref, update_ref, pair_ref, halves_ref, next_ref):
    rank = y_ref.shape[1]
    middle = z_ref[...] - dot3(split(y_ref[...]), split(update_ref[0]))
    pair = middle[:, :rank]
    pair_ref[...] = pair
    halves_ref[0], halves_ref[1] = split(pair)
    next_ref[...] = middle[:, rank:]


def final_kernel(mine_ref, other_ref, halves_ref, next_ref, out_ref):
    rank = mine_ref.shape[0]
    mine = split(mine_ref[:, :rank])
    other = split(other_ref[:, :rank])
    start = other_ref[:, rank:] - dot3(other, split(mine_ref[:, rank:]))
    update = start + dot3(other, split(dot3(mine, split(start))))
    out_ref[...] = next_ref[...] - dot3((halves_ref[0], halves_ref[1]), split(update))


def run(kernel, shapes, args, scratch=(), flops=0, space=pltpu.VMEM, limit=24 << 20):
    bytes_moved = sum(a.size * 4 for a in args) + sum(4 * s.size for s in shapes)
    return pl.pallas_call(
        kernel,
        out_shape=shapes,
        in_specs=[pl.BlockSpec(memory_space=space)] * len(args),
        out_specs=[pl.BlockSpec(memory_space=pltpu.VMEM)] * len(shapes),
        scratch_shapes=list(scratch),
        compiler_params=pltpu.CompilerParams(vmem_limit_bytes=limit),
        cost_estimate=pl.CostEstimate(flops=flops, bytes_accessed=bytes_moved, transcendentals=0),
    )(*args)


def array(*shape, dtype=jnp.float32):
    return jax.ShapeDtypeStruct(shape, dtype)


def after(x, *others):
    return lax.optimization_barrier((x, *others))[0]


def body(low_solved, low_basis, upper_solved, upper_basis):
    depth, rank = low_solved.shape
    leaves = lax.axis_size("leaf")
    bits = leaves.bit_length() - 2
    blocks = 1 << bits
    rows = rank // blocks
    unit = 6 * rank * rank

    half = array(blocks // 2, rows, 3 * rank)
    low_send, low_keep, joined = run(
        functools.partial(low_kernel, bits),
        [half, half, array(2, depth, 3 * rank, dtype=jnp.bfloat16)],
        [
            pltpu.with_memory_space_constraint(x, pltpu.HBM)
            for x in (low_solved, upper_solved, low_basis)
        ],
        [
            pltpu.VMEM((depth, rank), jnp.float32),
            pltpu.VMEM((depth, 2 * rank), jnp.float32),
            pltpu.VMEM((depth, rank), jnp.float32),
            pltpu.VMEM((rank, 3 * rank), jnp.float32),
            pltpu.SemaphoreType.DMA((2, 3)),
        ],
        flops=3 * unit * depth,
        space=pltpu.HBM,
    )
    high_send, high_keep = run(
        functools.partial(high_kernel, bits),
        [half, half],
        [upper_basis, joined],
        [pltpu.VMEM((rank, 3 * rank), jnp.float32)],
        flops=3 * unit * depth,
    )

    def merge(keep, got):
        half = keep.shape[0] // 2
        if half == 0:
            return keep[0] + got[0], None
        return keep[half:] + got[half:], keep[:half] + got[:half]

    def grow(x, got):
        return jnp.concatenate([x, got], axis=0)

    for t in range(bits):
        low_got = step(low_send, "low", t, bits, "scatter")
        high_got = step(high_send, "high", t, bits, "scatter")
        low_send, low_keep = merge(low_keep, after(low_got, high_send))
        high_send, high_keep = merge(high_keep, after(high_got, low_send))
    low_mine, high_mine = low_send, high_send
    with jax.named_scope("low_swap"):
        low_other = flip(low_mine, "leaf", bits)
    with jax.named_scope("high_swap"):
        high_other = flip(high_mine, "leaf", bits)

    other, own = low_other[None], after(low_mine, high_mine)[None]
    own = grow(own, after(step(own, "own", 0, bits, "gather"), other))
    high_other = after(high_other, own)
    both = [high_mine[:, :rank], high_other[:, :rank], high_mine[:, rank:] + high_other[:, rank:]]
    high = jnp.concatenate(both, axis=1)[None]
    for t in range(bits - 1):
        other_got = step(other, "other", t, bits, "gather")
        own_got = step(own, "own", t + 1, bits, "gather")
        high_got = step(high, "high", t, bits, "gather")
        other = grow(other, after(other_got, high))
        own_got = after(own_got, other)
        if t < bits - 2:
            own = grow(own, own_got)
        high = grow(high, after(high_got, own_got))
    low_parts = [own, own_got, other, step(other, "other", bits - 1, bits, "gather")]
    high_parts = [high, step(high, "high", bits - 1, bits, "gather")]

    (update,) = run(
        functools.partial(solve_kernel, bits),
        [array(2, rank, 2 * rank)],
        low_parts,
        [pltpu.VMEM((rank, 3 * rank), jnp.float32)] * 2,
        flops=36 * unit * rank,
    )
    (total,) = run(
        functools.partial(total_kernel, bits),
        [array(rank, 2 * rank)],
        [*high_parts, update],
        [pltpu.VMEM((rank, 4 * rank), jnp.float32)],
        flops=4 * unit * rank,
    )
    sibling = flip(total, "group", 0)
    pair_solved, halves, next_terms = run(
        middle_kernel,
        [array(depth, rank), array(2, depth, rank, dtype=jnp.bfloat16), array(depth, rank)],
        [low_solved, upper_solved, update],
        flops=2 * unit * depth,
    )
    (next_solved,) = run(
        final_kernel,
        [array(depth, rank)],
        [total, sibling, halves, next_terms],
        flops=3 * unit * rank + unit * depth,
    )
    return pair_solved, next_solved


def solution(mesh):
    spec = P(("group", "leaf"), None)
    return jax.shard_map(
        body,
        mesh=mesh,
        in_specs=(spec, spec, spec, spec),
        out_specs=(spec, spec),
        check_vma=False,
    )
```

```python
import functools

import jax
import jax.numpy as jnp
from jax import lax
from jax.experimental import pallas as pl
from jax.experimental.pallas import tpu as pltpu
from jax.sharding import PartitionSpec as P

AXES = ("leaf", "group")


def axis_order(chain, core, bits, stage):
    pair, rest = [core, 1 - core], list(range(2, bits))
    if stage == "scatter":
        return pair + rest if chain == "low" else rest + pair
    if chain == "high":
        return [1, 0] + rest if core == 0 else rest + [0, 1]
    return pair + rest if chain == "own" else rest + pair[::-1]


def relative_bits(order, r, first_is_high):
    bits = len(order)
    out = 0
    for t in range(bits):
        place = bits - 1 - t if first_is_high else t
        if (r >> place) & 1:
            out |= 1 << order[t]
    return out


def step(x, chain, t, bits, stage):
    leaves, groups = lax.axis_size("leaf"), lax.axis_size("group")
    pairs = []
    for leaf in range(leaves):
        for group in range(groups):
            bit = axis_order(chain, group % 2, bits, stage)[t]
            pairs.append((leaf * groups + group, (leaf ^ (1 << bit)) * groups + group))
    with jax.named_scope(f"{chain}_{stage}_{t}"):
        return lax.ppermute(x, AXES, pairs)


def flip(x, axis, bit):
    return lax.ppermute(x, axis, [(i, i ^ (1 << bit)) for i in range(lax.axis_size(axis))])


def split(x):
    high = x.astype(jnp.bfloat16)
    low = (x - high.astype(jnp.float32)).astype(jnp.bfloat16)
    return high, low


def dot3(left, right, dims=(((1,), (0,)), ((), ()))):
    dot = functools.partial(
        lax.dot_general, dimension_numbers=dims, preferred_element_type=jnp.float32
    )
    return dot(left[0], right[0]) + (dot(left[0], right[1]) + dot(left[1], right[0]))


def block_of(r, chain, bits, stage):
    orders = [axis_order(chain, core, bits, stage) for core in range(2)]
    moves = [relative_bits(order, r, stage == "scatter") for order in orders]
    own = lax.rem(lax.axis_index("leaf"), 1 << bits)
    core = lax.rem(lax.axis_index("group"), 2)
    return lax.bitwise_xor(own, jnp.where(core == 0, moves[0], moves[1]))


def hand_out(sums, chain, bits, send_ref, keep_ref):
    blocks = 1 << bits
    rows = sums.shape[0] // blocks
    for r in range(blocks):
        start = pl.multiple_of(block_of(r, chain, bits, "scatter") * rows, rows)
        target = send_ref if r >= blocks // 2 else keep_ref
        target[r % (blocks // 2)] = sums[pl.ds(start, rows), :]


def low_kernel(bits, *refs):
    inputs, (send_ref, keep_ref, joined) = refs[:3], refs[3:6]
    loaded, (sums, sems) = refs[6:9], refs[9:]
    depth, rank = inputs[0].shape
    parts = sems.shape[0]
    part = depth // parts
    copies = [
        [
            pltpu.make_async_copy(
                source.at[pl.ds(p * part, part)], target.at[pl.ds(p * part, part)], sems.at[p, i]
            )
            for i, (source, target) in enumerate(zip(inputs, loaded))
        ]
        for p in range(parts)
    ]
    for group in copies:
        for copy in group:
            copy.start()
    y, z, basis = loaded
    dims = (((0,), (0,)), ((), ()))
    for p in range(parts):
        span = pl.ds(p * part, part)
        for copy in copies[p]:
            copy.wait()
        for source, columns in ((y, pl.ds(0, rank)), (z, pl.ds(rank, 2 * rank))):
            high, low = split(source[span, :])
            joined[0, span, columns] = high
            joined[1, span, columns] = low
        term = dot3(split(basis[span, :]), (joined[0, span, :], joined[1, span, :]), dims)
        sums[...] = term if p == 0 else sums[...] + term
    hand_out(sums, "low", bits, send_ref, keep_ref)


def high_kernel(bits, basis_ref, joined, send_ref, keep_ref, sums):
    dims = (((0,), (0,)), ((), ()))
    sums[...] = dot3(split(basis_ref[...]), (joined[0], joined[1]), dims)
    hand_out(sums, "high", bits, send_ref, keep_ref)


def place(parts, chain, bits, target):
    blocks = 1 << bits
    rows = target.shape[0] // blocks
    for r in range(blocks):
        start = pl.multiple_of(block_of(r, chain, bits, "gather") * rows, rows)
        target[pl.ds(start, rows), :] = parts[r // (blocks // 2)][r % (blocks // 2)]


def solve_kernel(bits, own_low, own_high, other_low, other_high, update_ref, own, other):
    rank = update_ref.shape[1]
    place((own_low, own_high), "own", bits, own)
    place((other_low, other_high), "other", bits, other)
    terms = (own, other)
    couples = [split(x[:, :rank]) for x in terms]
    for i in range(2):
        mine, far = couples[i], couples[1 - i]
        start = terms[1 - i][:, rank:] - dot3(far, split(terms[i][:, rank:]))
        update_ref[i] = start + dot3(far, split(dot3(mine, split(start))))


def total_kernel(bits, first_ref, second_ref, update_ref, total_ref, terms):
    rank = total_ref.shape[0]
    place((first_ref, second_ref), "high", bits, terms)
    total = terms[:, 2 * rank :]
    for i in range(2):
        total = total - dot3(split(terms[:, i * rank : (i + 1) * rank]), split(update_ref[i]))
    total_ref[...] = total


def middle_kernel(joined, update_ref, pair_ref, halves_ref, next_ref):
    rank = pair_ref.shape[1]
    y = (joined[0, :, :rank], joined[1, :, :rank])
    z = joined[0, :, rank:].astype(jnp.float32) + joined[1, :, rank:].astype(jnp.float32)
    middle = z - dot3(y, split(update_ref[0]))
    pair = middle[:, :rank]
    pair_ref[...] = pair
    halves_ref[0], halves_ref[1] = split(pair)
    next_ref[...] = middle[:, rank:]


def final_kernel(mine_ref, other_ref, halves_ref, next_ref, out_ref):
    rank = mine_ref.shape[0]
    mine = split(mine_ref[:, :rank])
    other = split(other_ref[:, :rank])
    start = other_ref[:, rank:] - dot3(other, split(mine_ref[:, rank:]))
    update = start + dot3(other, split(dot3(mine, split(start))))
    out_ref[...] = next_ref[...] - dot3((halves_ref[0], halves_ref[1]), split(update))


def run(kernel, shapes, args, scratch=(), flops=0, space=pltpu.VMEM, limit=24 << 20):
    bytes_moved = sum(a.size * 4 for a in args) + sum(4 * s.size for s in shapes)
    return pl.pallas_call(
        kernel,
        out_shape=shapes,
        in_specs=[pl.BlockSpec(memory_space=space)] * len(args),
        out_specs=[pl.BlockSpec(memory_space=pltpu.VMEM)] * len(shapes),
        scratch_shapes=list(scratch),
        compiler_params=pltpu.CompilerParams(vmem_limit_bytes=limit),
        cost_estimate=pl.CostEstimate(flops=flops, bytes_accessed=bytes_moved, transcendentals=0),
    )(*args)


def array(*shape, dtype=jnp.float32):
    return jax.ShapeDtypeStruct(shape, dtype)


def after(x, *others):
    return lax.optimization_barrier((x, *others))[0]


def body(low_solved, low_basis, upper_solved, upper_basis):
    depth, rank = low_solved.shape
    leaves = lax.axis_size("leaf")
    bits = leaves.bit_length() - 2
    blocks = 1 << bits
    rows = rank // blocks
    unit = 6 * rank * rank

    half = array(blocks // 2, rows, 3 * rank)
    low_send, low_keep, joined = run(
        functools.partial(low_kernel, bits),
        [half, half, array(2, depth, 3 * rank, dtype=jnp.bfloat16)],
        [
            pltpu.with_memory_space_constraint(x, pltpu.HBM)
            for x in (low_solved, upper_solved, low_basis)
        ],
        [
            pltpu.VMEM((depth, rank), jnp.float32),
            pltpu.VMEM((depth, 2 * rank), jnp.float32),
            pltpu.VMEM((depth, rank), jnp.float32),
            pltpu.VMEM((rank, 3 * rank), jnp.float32),
            pltpu.SemaphoreType.DMA((2, 3)),
        ],
        flops=3 * unit * depth,
        space=pltpu.HBM,
    )
    high_send, high_keep = run(
        functools.partial(high_kernel, bits),
        [half, half],
        [upper_basis, joined],
        [pltpu.VMEM((rank, 3 * rank), jnp.float32)],
        flops=3 * unit * depth,
    )

    def merge(keep, got):
        half = keep.shape[0] // 2
        if half == 0:
            return keep[0] + got[0], None
        return keep[half:] + got[half:], keep[:half] + got[:half]

    def grow(x, got):
        return jnp.concatenate([x, got], axis=0)

    for t in range(bits):
        low_got = step(low_send, "low", t, bits, "scatter")
        high_got = step(high_send, "high", t, bits, "scatter")
        low_send, low_keep = merge(low_keep, after(low_got, high_send))
        high_send, high_keep = merge(high_keep, after(high_got, low_send))
    low_mine, high_mine = low_send, high_send
    with jax.named_scope("low_swap"):
        low_other = flip(low_mine, "leaf", bits)
    with jax.named_scope("high_swap"):
        high_other = flip(high_mine, "leaf", bits)

    other, own = low_other[None], after(low_mine, high_mine)[None]
    own = grow(own, after(step(own, "own", 0, bits, "gather"), other))
    high_other = after(high_other, own)
    both = [high_mine[:, :rank], high_other[:, :rank], high_mine[:, rank:] + high_other[:, rank:]]
    high = jnp.concatenate(both, axis=1)[None]
    for t in range(bits - 1):
        other_got = step(other, "other", t, bits, "gather")
        own_got = step(own, "own", t + 1, bits, "gather")
        high_got = step(high, "high", t, bits, "gather")
        other = grow(other, after(other_got, high))
        own_got = after(own_got, other)
        if t < bits - 2:
            own = grow(own, own_got)
        high = grow(high, after(high_got, own_got))
    low_parts = [own, own_got, other, step(other, "other", bits - 1, bits, "gather")]
    high_parts = [high, step(high, "high", bits - 1, bits, "gather")]

    (update,) = run(
        functools.partial(solve_kernel, bits),
        [array(2, rank, 2 * rank)],
        low_parts,
        [pltpu.VMEM((rank, 3 * rank), jnp.float32)] * 2,
        flops=36 * unit * rank,
    )
    (total,) = run(
        functools.partial(total_kernel, bits),
        [array(rank, 2 * rank)],
        [*high_parts, update],
        [pltpu.VMEM((rank, 4 * rank), jnp.float32)],
        flops=4 * unit * rank,
    )
    sibling = flip(total, "group", 0)
    pair_solved, halves, next_terms = run(
        middle_kernel,
        [array(depth, rank), array(2, depth, rank, dtype=jnp.bfloat16), array(depth, rank)],
        [joined, update],
        flops=2 * unit * depth,
    )
    (next_solved,) = run(
        final_kernel,
        [array(depth, rank)],
        [total, sibling, halves, next_terms],
        flops=3 * unit * rank + unit * depth,
    )
    return pair_solved, next_solved


def solution(mesh):
    spec = P(("group", "leaf"), None)
    return jax.shard_map(
        body,
        mesh=mesh,
        in_specs=(spec, spec, spec, spec),
        out_specs=(spec, spec),
        check_vma=False,
    )
```
